32 devices in a mesh: groups: 2 (over y), seq: 8 (over z, x), batch: 2 (over core).
Axes of the slice: x: 2, y: 2, z: 4, core: 2. Of those that a mesh axis runs over, the one named last changes fastest.
Arguments:
- x_in: bfloat16 [4, 512, 2560], P(('groups', 'batch'), 'seq'), parts along dimension 0, may hold values from -6 to 6
- b_in: bfloat16 [4, 512, 128], P(('groups', 'batch'), 'seq'), parts along dimension 0, may hold values from -0.1875 to 0.1875
- c_in: bfloat16 [4, 512, 128], P(('groups', 'batch'), 'seq'), parts along dimension 0, may hold values from -6 to 6
- log_decay: float32 [4, 40, 512], P(('groups', 'batch'), None, 'seq'), parts along dimension 0, may hold values from -0.8 to 0, as said below
- skip: float32 [40], replicated, may hold values from 0.5 to 4
- norm_gain: float32 [2560], replicated, may hold values from 0.1 to 1.9
- queries: bfloat16 [4, 512, 512], P(('groups', 'batch'), 'seq'), parts along dimension 0, may hold values from -60 to 60
- keys: bfloat16 [4, 512, 512], P(('groups', 'batch'), 'seq'), parts along dimension 0, may hold values from -4 to 4
Outputs:
- scan_out: bfloat16 [4, 512, 2560], P(('groups', 'batch'), 'seq'), parts along dimension 0
- attended: bfloat16 [4, 512, 512], P(('groups', 'batch'), 'seq'), parts along dimension 0
The draws below stay inside these ranges and needn't reach their ends.
There are 2 independent parts, one for each index of `groups`. The reference program is written for one: setup_inputs(seed, part) draws one part's arguments, and reference() takes and returns one part's arrays. A program takes and returns all parts, laid end to end along the dimension named above; an argument that names none is the same for every part. Nothing has to cross between parts.
Inputs may be any that keep to these rules, and one draw needn't show every extreme that they name: log_decay is never positive.
All inputs are finite; a program needn't handle non-finite values.
Results may differ from the reference program's by a relative error of at most 0.0051.
Values may be sent and summed in bfloat16 or wider, within the bound.
A program may use at most 128 MiB of HBM per device.

```python
import math
import jax
import jax.numpy as jnp
from jax import lax

HEAD_DIM = 64
STATE = 128
SSM_HEADS = 40
SPAN = 64
ATT_HEADS = 8
SEQ_LEN = 512
SEQS = 2


def key_values(key):
    base = jax.random.fold_in(key, 7)
    shape = (SEQS, SEQ_LEN, ATT_HEADS * HEAD_DIM)
    vals = jnp.clip(jax.random.normal(base, shape, jnp.float32), -4.0, 4.0)
    return vals


def draw_keys(key, part):
    return key_values(key).astype(jnp.bfloat16)


def draw_queries(key, part):
    base = jax.random.fold_in(key, 13)
    shape = (SEQS, SEQ_LEN, ATT_HEADS * HEAD_DIM)
    vals = 2.5 * jnp.clip(jax.random.normal(base, shape, jnp.float32), -4.0, 4.0)
    return vals.astype(jnp.bfloat16)


def draw_log_decay(key, part):
    shape = (SEQS, SSM_HEADS, SEQ_LEN)
    k_rate, k_jitter, k_spots, k_drop = jax.random.split(jax.random.fold_in(key, 29), 4)
    lowest = 0.05 / SEQ_LEN
    highest = 1.0 / 30.0
    rate = jnp.exp(jax.random.uniform(k_rate, (SEQS, SSM_HEADS, 1), jnp.float32, jnp.log(lowest), jnp.log(highest)))
    jitter = jnp.exp(jax.random.uniform(k_jitter, shape, jnp.float32, jnp.log(0.5), jnp.log(2.0)))
    spots = jax.random.randint(k_spots, (SEQS, 1, 1, 3), 0, SEQ_LEN)
    places = jnp.arange(SEQ_LEN)[None, None, :, None]
    struck = jnp.any(places == spots, axis=-1)
    drop = jnp.log(jax.random.uniform(k_drop, shape, jnp.float32, 0.5, 0.8))
    return -rate * jitter + jnp.where(struck, drop, 0.0)


def shard_levels(own_key, extent, cuts, smallest, top_value):
    factor_of = 1.0
    for dim, parts in cuts:
        heights = jax.random.uniform(jax.random.fold_in(jax.random.fold_in(own_key, 6), dim), (parts,), jnp.float32, smallest / len(cuts), top_value / len(cuts))
        factor_of = factor_of * jnp.repeat(jnp.exp(heights), extent[dim] // parts).reshape((-1,) + (1,) * (len(extent) - 1 - dim))
    return factor_of


def scatter_about(rng, dims, spread, limit, cuts=(), kind=jnp.bfloat16):
    drawn = jax.random.normal(rng, dims, jnp.float32) * spread
    if len(cuts) > 0:
        drawn = shard_levels(rng, dims, cuts, -0.22, 0.18) * drawn
    return jnp.clip(drawn, min=-limit, max=limit).astype(kind)


def setup_inputs(seed: int = 0, part: int = 0) -> dict:
    key_list = jax.random.split(jax.random.key(seed), 9)
    part_splits = jax.random.split(jax.random.fold_in(key_list[8], part), 9)
    return {
        "x_in": scatter_about(part_splits[0], (SEQS, SEQ_LEN, SSM_HEADS * HEAD_DIM), 1.0, 6.0, ((0, 2), (1, 8))),
        "b_in": scatter_about(part_splits[1], (SEQS, SEQ_LEN, STATE), (8.0 * (STATE * SEQ_LEN) ** -0.5), 0.1875, ((0, 2), (1, 8))),
        "c_in": scatter_about(part_splits[2], (SEQS, SEQ_LEN, STATE), 1.0, 6.0, ((0, 2), (1, 8))),
        "log_decay": draw_log_decay(jax.random.fold_in(jax.random.fold_in(key_list[8], part), 71), part),
        "skip": jnp.clip(jnp.exp(jax.random.uniform(key_list[4], (SSM_HEADS,), jnp.float32, math.log(0.5), math.log(4.0))), 0.5, 4.0),
        "norm_gain": jnp.clip(1.0 + 0.18 * jax.random.normal(key_list[5], (SSM_HEADS * HEAD_DIM,), jnp.float32), 0.1, 1.9),
        "queries": draw_queries(jax.random.fold_in(jax.random.fold_in(key_list[8], part), 71), part),
        "keys": draw_keys(jax.random.fold_in(jax.random.fold_in(key_list[8], part), 71), part),
    }


HIGH = lax.Precision.HIGHEST

def attend_one(pieces):
    query_rows, key_rows, value_rows = pieces
    qf = query_rows.astype(jnp.float32)
    kf = key_rows.astype(jnp.float32)
    vf = value_rows.astype(jnp.float32)
    length = qf.shape[0]
    block = min(512, length)
    count = length // block
    scale = HEAD_DIM ** (-0.5)

    def one_block(index):
        start = index * block
        part = lax.dynamic_slice_in_dim(qf, start, block, 0)
        scores = jnp.dot(part, kf.T, precision=HIGH) * scale
        rows = start + jnp.arange(block, dtype=jnp.int32)
        cols = jnp.arange(length, dtype=jnp.int32)
        mask = cols[None, :] <= rows[:, None]
        scores = jnp.where(mask, scores, -jnp.inf)
        top = lax.optimization_barrier(jnp.max(scores, axis=-1, keepdims=True))
        probs = jnp.exp(scores - top)
        total = lax.optimization_barrier(jnp.sum(probs, axis=-1, keepdims=True))
        rounded = lax.optimization_barrier(probs.astype(jnp.bfloat16)).astype(jnp.float32)
        mixed = jnp.dot(rounded, vf, precision=HIGH) / total
        return mixed.astype(jnp.bfloat16)
    blocks = lax.map(one_block, jnp.arange(count, dtype=jnp.int32))
    return blocks.reshape(length, HEAD_DIM)

def reference(x_in, b_in, c_in, log_decay, skip, norm_gain, queries, keys):
    nchunk = SEQ_LEN // SPAN
    xr = x_in.astype(jnp.float32).reshape(SEQS, nchunk, SPAN, SSM_HEADS, HEAD_DIM).transpose(1, 0, 2, 3, 4)
    br = b_in.astype(jnp.float32).reshape(SEQS, nchunk, SPAN, STATE).transpose(1, 0, 2, 3)
    cr = c_in.astype(jnp.float32).reshape(SEQS, nchunk, SPAN, STATE).transpose(1, 0, 2, 3)
    rates = log_decay.reshape(SEQS, SSM_HEADS, nchunk, SPAN).transpose(2, 0, 1, 3)
    lower = jnp.arange(SPAN)[:, None] >= jnp.arange(SPAN)[None, :]

    def advance(carry, pieces):
        xs, bs, cs_, rate = pieces
        cum = jnp.cumsum(rate, axis=-1)
        inner = jnp.einsum('btn,bsn->bts', cs_, bs, precision=HIGH)
        weights = jnp.where(lower, jnp.exp(cum[..., :, None] - cum[..., None, :]), 0.0)
        weighted = inner[:, None, :, :] * weights
        intra = jnp.einsum('bhts,bshp->bthp', weighted, xs, precision=HIGH)
        reach = jnp.transpose(jnp.exp(cum), (0, 2, 1))[..., None]
        state_part = reach * jnp.einsum('btn,bhpn->bthp', cs_, carry, precision=HIGH)
        result = intra + state_part + skip[None, None, :, None] * xs
        tail = jnp.exp(cum[..., -1:] - cum)
        fresh = jnp.einsum('bhs,bshp,bsn->bhpn', tail, xs, bs, precision=HIGH)
        carry = jnp.exp(cum[..., -1])[..., None, None] * carry + fresh
        return (carry, result)
    start = jnp.zeros((SEQS, SSM_HEADS, HEAD_DIM, STATE), jnp.float32)
    _, outs = lax.scan(advance, start, (xr, br, cr, rates))
    y = outs.transpose(1, 0, 2, 3, 4).reshape(SEQS, SEQ_LEN, SSM_HEADS, HEAD_DIM)
    mean_sq = lax.optimization_barrier(jnp.mean(y * y, axis=-1, keepdims=True))
    normed = y * lax.rsqrt(mean_sq + 1e-05) * norm_gain.reshape(SSM_HEADS, HEAD_DIM)
    scan_out = normed.astype(jnp.bfloat16).reshape(SEQS, SEQ_LEN, SSM_HEADS * HEAD_DIM)
    values = scan_out[:, :, :ATT_HEADS * HEAD_DIM]

    def by_head(arr):
        return arr.reshape(SEQS, SEQ_LEN, ATT_HEADS, HEAD_DIM).transpose(0, 2, 1, 3).reshape(SEQS * ATT_HEADS, SEQ_LEN, HEAD_DIM)
    mixed = lax.map(attend_one, (by_head(queries), by_head(keys), by_head(values)))
    attended = mixed.reshape(SEQS, ATT_HEADS, SEQ_LEN, HEAD_DIM).transpose(0, 2, 1, 3).reshape(SEQS, SEQ_LEN, ATT_HEADS * HEAD_DIM)
    return (scan_out, attended)
```

```python
import functools
import math
import jax
import jax.numpy as jnp
from jax import lax
from jax.sharding import PartitionSpec as P
from jax.experimental import pallas as pl
from jax.experimental.pallas import tpu as pltpu

F32 = jnp.float32
BF16 = jnp.bfloat16
HIGH = lax.Precision.HIGHEST
LOG2E = math.log2(math.e)
MESH = pl.DeviceIdType.MESH
BC, LD, QK, ATT, FIXED = 0, 1, 2, 3, 4


def lanes(a, b):
    return jnp.concatenate([a, b], axis=1)


def rows(parts):
    return jnp.concatenate(parts, axis=0)


def kernel(n, tok, heads, dim, per, blk,
           x_ref, b_ref, c_ref, ld_ref, skip_ref, gain_ref, q_ref, k_ref,
           out_ref, att_ref,
           xs, xr, qks, qkr, bcs, bcr, lds, ldr, ys, yr, ats, atr, inner, send, recv):
    me = lax.axis_index("seq")
    half = tok // 2
    slots = xs.shape[1]
    length = n * tok
    nblk = length // blk

    barrier = pltpu.get_barrier_semaphore()

    def greet(k, _):
        pl.semaphore_signal(barrier, inc=1, device_id={"seq": lax.rem(me + k, n)}, device_id_type=MESH)
        return 0

    lax.fori_loop(1, n, greet, 0)

    def copy(src, dst, row, k):
        return pltpu.make_async_remote_copy(
            src_ref=src, dst_ref=dst, send_sem=send.at[row, k], recv_sem=recv.at[row, k],
            device_id={"seq": lax.rem(me + k, n)}, device_id_type=MESH)

    def to(k):
        return lax.rem(me + k, n)

    def each(fn):
        def body(k, _):
            fn(k)
            return 0
        lax.fori_loop(1, n, body, 0)

    bc_copy = lambda k: copy(bcs, bcr.at[me], BC, k)
    ld_copy = lambda k: copy(lds.at[to(k)], ldr.at[me], LD, k)
    qk_copy = lambda k: copy(qks.at[to(k)], qkr.at[me], QK, k)
    att_copy = lambda k: copy(ats.at[to(k)], atr.at[me], ATT, k)
    x_copy = lambda slot: lambda k: copy(xs.at[to(k), slot], xr.at[me, slot], FIXED + slot, k)
    y_copy = lambda slot: lambda k: copy(ys.at[to(k), slot], yr.at[me, slot], FIXED + slots + slot, k)
    start = lambda mk: each(lambda k: mk(k).start())
    arrive = lambda mk: each(lambda k: mk(k).wait_recv())
    left = lambda mk: each(lambda k: mk(k).wait_send())

    bcs[0:tok] = b_ref[0]
    bcs[tok:] = c_ref[0]
    bcr[me] = bcs[...]
    upper = (lax.broadcasted_iota(jnp.int32, (tok, tok), 0)
             <= lax.broadcasted_iota(jnp.int32, (tok, tok), 1)).astype(F32)
    sums = jnp.dot(ld_ref[0], upper, precision=HIGH, preferred_element_type=F32) * LOG2E
    lds[...] = jnp.zeros_like(lds)
    for slot in range(slots):
        count = min(n, heads - slot * n)
        lds[0:count, slot, 0:tok] = sums[slot * n : slot * n + count]
    ldr[me] = lds[me]

    def pack(src, head_of, store):
        for p in range(src.shape[2] // (2 * dim)):
            t = src[0, :, p * 2 * dim : (p + 1) * 2 * dim]
            top, bot = t[:half], t[half:]
            store(2 * p, lanes(top[:, :dim], bot[:, :dim]))
            store(2 * p + 1, lanes(top[:, dim:], bot[:, dim:]))

    def x_slot(slot):
        for p in range(n // 2):
            h = slot * n + 2 * p
            if h < heads:
                t = x_ref[0, :, h * dim : (h + 2) * dim]
                top, bot = t[:half], t[half:]
                xs[2 * p, slot] = lanes(top[:, :dim], bot[:, :dim])
                xs[2 * p + 1, slot] = lanes(top[:, dim:], bot[:, dim:])
            else:
                xs[2 * p, slot] = jnp.zeros((half, 2 * dim), BF16)
                xs[2 * p + 1, slot] = jnp.zeros((half, 2 * dim), BF16)
        xr[me, slot] = xs[me, slot]

    def qk_slot():
        for which, src in enumerate((q_ref, k_ref)):
            for p in range(per * n // 2):
                t = src[0, :, p * 2 * dim : (p + 1) * 2 * dim]
                top, bot = t[:half], t[half:]
                h = 2 * p
                qks[h % n, 2 * (h // n) + which] = lanes(top[:, :dim], bot[:, :dim])
                h = 2 * p + 1
                qks[h % n, 2 * (h // n) + which] = lanes(top[:, dim:], bot[:, dim:])
        qkr[me] = qks[me]

    pl.semaphore_wait(barrier, n - 1)
    start(bc_copy)
    start(ld_copy)
    x_slot(0)
    start(x_copy(0))
    qk_slot()
    start(qk_copy)
    for slot in range(1, slots):
        x_slot(slot)
        start(x_copy(slot))

    def unpack(ref, index):
        parts = []
        for c in range(n):
            t = ref[c, index]
            parts += [t[:, :dim], t[:, dim:]]
        return rows(parts)

    def packed(a):
        return lanes(a[:half], a[half:])

    arrive(bc_copy)
    b_all = bcr[:, 0:tok, :].reshape(length, bcr.shape[2])
    for i in range(nblk):
        if blk % tok == 0:
            c_i = bcr[i * (blk // tok) : (i + 1) * (blk // tok), tok:, :].reshape(blk, bcr.shape[2])
        inner[i * blk : (i + 1) * blk, 0 : (i + 1) * blk] = lax.dot_general(
            c_i, b_all[: (i + 1) * blk], (((1,), (1,)), ((), ())), preferred_element_type=F32)
    arrive(ld_copy)
    offset = jnp.zeros((ldr.shape[1], 1), F32)
    parts = []
    for c in range(n):
        part = ldr[c][:, :tok] + offset
        offset = part[:, tok - 1 : tok]
        parts.append(part)
    cum = jnp.concatenate(parts, axis=1)
    cum_t = cum.T

    lower = (lax.broadcasted_iota(jnp.int32, (blk, blk), 0)
             >= lax.broadcasted_iota(jnp.int32, (blk, blk), 1))

    def attend(slot, values):
        q = unpack(qkr, 2 * slot)
        key = unpack(qkr, 2 * slot + 1)
        for i in range(nblk):
            s = lax.dot_general(q[i * blk : (i + 1) * blk], key[: (i + 1) * blk],
                                (((1,), (1,)), ((), ())), preferred_element_type=F32)
            s = s * (dim ** -0.5 * LOG2E)
            diag = jnp.where(lower, s[:, i * blk :], -jnp.inf)
            s = diag if i == 0 else lanes(s[:, : i * blk], diag)
            top = jnp.max(s, axis=-1, keepdims=True)
            w = jnp.exp2(s - top)
            total = jnp.sum(w, axis=-1, keepdims=True)
            mixed = jnp.dot(w.astype(BF16), values[: (i + 1) * blk], preferred_element_type=F32) / total
            mixed = mixed.astype(BF16)
            for c in range(blk // tok):
                ats[i * (blk // tok) + c, slot] = packed(mixed[c * tok : (c + 1) * tok])

    for slot in range(slots):
        head = jnp.minimum(me + slot * n, heads - 1)
        arrive(x_copy(slot))
        x_all = unpack(xr, slot)
        skip = skip_ref[head]
        pair = gain_ref[pl.ds(head // 2, 1), :]
        gain = jnp.where(head % 2 == 0, pair[:, :dim], pair[:, dim:])
        outs = []
        for i in range(nblk):
            here = cum_t[i * blk : (i + 1) * blk, slot : slot + 1]
            w = here - cum[slot : slot + 1, : (i + 1) * blk]
            diag = jnp.where(lower, w[:, i * blk :], -jnp.inf)
            w = diag if i == 0 else lanes(w[:, : i * blk], diag)
            w = jnp.exp2(w) * inner[i * blk : (i + 1) * blk, : (i + 1) * blk]
            y = jnp.dot(w.astype(BF16), x_all[: (i + 1) * blk], preferred_element_type=F32)
            y = y + skip * x_all[i * blk : (i + 1) * blk].astype(F32)
            mean = jnp.mean(y * y, axis=-1, keepdims=True)
            y = (y * lax.rsqrt(mean + 1e-05) * gain).astype(BF16)
            for c in range(blk // tok):
                ys[i * (blk // tok) + c, slot] = packed(y[c * tok : (c + 1) * tok])
            outs.append(y)
        start(y_copy(slot))
        yr[me, slot] = ys[me, slot]
        if slot < per:
            if slot == 0:
                arrive(qk_copy)
            attend(slot, rows(outs))
            if slot == per - 1:
                start(att_copy)
                atr[me] = ats[me]

    def unpack_out(ref, slot, dst):
        for p in range(n // 2):
            h = slot * n + 2 * p
            if h * dim < dst.shape[2]:
                even, odd = ref[2 * p, slot], ref[2 * p + 1, slot]
                dst[0, :half, h * dim : (h + 2) * dim] = lanes(even[:, :dim], odd[:, :dim])
                dst[0, half:, h * dim : (h + 2) * dim] = lanes(even[:, dim:], odd[:, dim:])

    for slot in range(slots):
        arrive(y_copy(slot))
        unpack_out(yr, slot, out_ref)
        if slot == per - 1:
            arrive(att_copy)
            for a in range(per):
                unpack_out(atr, a, att_ref)

    left(bc_copy)
    left(ld_copy)
    left(qk_copy)
    left(att_copy)
    for slot in range(slots):
        left(x_copy(slot))
        left(y_copy(slot))


def local(n, x_in, b_in, c_in, log_decay, skip, norm_gain, queries, keys):
    tok, width = x_in.shape[1:]
    heads = log_decay.shape[1]
    dim = width // heads
    state = b_in.shape[2]
    per = queries.shape[2] // dim // n
    slots = -(-heads // n)
    length = n * tok
    blk = 128 if length <= 512 else 256
    half = tok // 2
    pad = -(-slots // 8) * 8
    vmem = pl.BlockSpec(memory_space=pltpu.VMEM)
    smem = pl.BlockSpec(memory_space=pltpu.SMEM)
    block = lambda k: pltpu.VMEM((n, k, half, 2 * dim), BF16)
    rows_of = FIXED + 2 * slots
    return pl.pallas_call(
        functools.partial(kernel, n, tok, heads, dim, per, blk),
        out_shape=(jax.ShapeDtypeStruct(x_in.shape, BF16), jax.ShapeDtypeStruct(queries.shape, BF16)),
        in_specs=[vmem, vmem, vmem, vmem, smem, vmem, vmem, vmem],
        out_specs=(vmem, vmem),
        scratch_shapes=[
            block(slots), block(slots), block(2 * per), block(2 * per),
            pltpu.VMEM((2 * tok, state), BF16), pltpu.VMEM((n, 2 * tok, state), BF16),
            pltpu.VMEM((n, pad, 128), F32), pltpu.VMEM((n, pad, 128), F32),
            block(slots), block(slots), block(per), block(per),
            pltpu.VMEM((length, length), F32),
            pltpu.SemaphoreType.DMA((rows_of, n)), pltpu.SemaphoreType.DMA((rows_of, n)),
        ],
        compiler_params=pltpu.CompilerParams(
            collective_id=0, has_side_effects=True, vmem_limit_bytes=48 * 1024 * 1024),
    )(x_in, b_in, c_in, log_decay, skip, norm_gain.reshape(width // (2 * dim), 2 * dim), queries, keys)


def solution(mesh):
    rows_spec = P(("groups", "batch"), "seq", None)
    return jax.shard_map(
        functools.partial(local, mesh.shape["seq"]),
        mesh=mesh,
        in_specs=(rows_spec, rows_spec, rows_spec, P(("groups", "batch"), None, "seq"),
                  P(), P(), rows_spec, rows_spec),
        out_specs=(rows_spec, rows_spec),
        check_vma=False,
    )
```

```python
import functools
import math
import jax
import jax.numpy as jnp
from jax import lax
from jax.sharding import PartitionSpec as P
from jax.experimental import pallas as pl
from jax.experimental.pallas import tpu as pltpu

F32 = jnp.float32
BF16 = jnp.bfloat16
HIGH = lax.Precision.HIGHEST
LOG2E = math.log2(math.e)
MESH = pl.DeviceIdType.MESH
BC, LD, QK, ATT, FWD, FIXED = 0, 1, 2, 3, 4, 5


def lanes(a, b):
    return jnp.concatenate([a, b], axis=1)


def rows(parts):
    return jnp.concatenate(parts, axis=0)


def kernel(n, tok, heads, dim, per, blk,
           x_hbm, b_hbm, c_hbm, ld_hbm, skip_ref, gain_hbm, q_hbm, k_hbm,
           out_ref, att_ref,
           x_ref, ld_ref, gain_ref, q_ref, k_ref, load, xs, xr, qks, qkr, bcs, bcr, lds, ldr, ys, yr, ats, atr, inner, send, recv):
    me = lax.axis_index("seq")
    half = tok // 2
    slots = xs.shape[1]
    length = n * tok
    nblk = length // blk

    loads = [pltpu.make_async_copy(src, dst, load.at[i]) for i, (src, dst) in enumerate((
        (b_hbm.at[0], bcs.at[0:tok]), (c_hbm.at[0], bcs.at[tok : 2 * tok]), (ld_hbm, ld_ref), (x_hbm, x_ref),
        (q_hbm, q_ref), (k_hbm, k_ref), (gain_hbm, gain_ref)))]
    for one in loads:
        one.start()
    barrier = pltpu.get_barrier_semaphore()

    def greet(k, _):
        pl.semaphore_signal(barrier, inc=1, device_id={"seq": lax.rem(me + k, n)}, device_id_type=MESH)
        return 0

    lax.fori_loop(1, n, greet, 0)

    def copy(src, dst, row, k):
        return pltpu.make_async_remote_copy(
            src_ref=src, dst_ref=dst, send_sem=send.at[row, k], recv_sem=recv.at[row, k],
            device_id={"seq": lax.rem(me + k, n)}, device_id_type=MESH)

    def to(k):
        return lax.rem(me + k, n)

    def each(fn):
        def body(k, _):
            fn(k)
            return 0
        lax.fori_loop(1, n, body, 0)

    partner = me + 1 - 2 * lax.rem(me, 2)

    def bc_partner():
        return pltpu.make_async_remote_copy(
            src_ref=bcs, dst_ref=bcr.at[me], send_sem=send.at[BC, 1], recv_sem=recv.at[BC, 1],
            device_id={"seq": partner}, device_id_type=MESH)

    def bc_forward(k):
        slot = lax.rem(me + n - k, n)
        return pltpu.make_async_remote_copy(
            src_ref=bcr.at[slot], dst_ref=bcr.at[slot], send_sem=send.at[FWD, k], recv_sem=recv.at[FWD, k],
            device_id={"seq": partner}, device_id_type=MESH)

    def evens(fn):
        def body(j, _):
            fn(2 * j)
            return 0
        lax.fori_loop(1, n // 2, body, 0)

    def bc_relay(k):
        bc_copy(k).wait_recv()
        bc_forward(k).start()

    bc_copy = lambda k: copy(bcs, bcr.at[me], BC, k)
    ld_copy = lambda k: copy(lds.at[to(k)], ldr.at[me], LD, k)
    qk_copy = lambda k: copy(qks.at[to(k)], qkr.at[me], QK, k)
    att_copy = lambda k: copy(ats.at[to(k)], atr.at[me], ATT, k)
    x_copy = lambda slot: lambda k: copy(xs.at[to(k), slot], xr.at[me, slot], FIXED + slot, k)
    y_copy = lambda slot: lambda k: copy(ys.at[to(k), slot], yr.at[me, slot], FIXED + slots + slot, k)
    start = lambda mk: each(lambda k: mk(k).start())
    arrive = lambda mk: each(lambda k: mk(k).wait_recv())
    left = lambda mk: each(lambda k: mk(k).wait_send())

    lds[...] = jnp.zeros_like(lds)
    for one in loads[:3]:
        one.wait()
    bcr[me] = bcs[...]
    upper = (lax.broadcasted_iota(jnp.int32, (tok, tok), 0)
             <= lax.broadcasted_iota(jnp.int32, (tok, tok), 1)).astype(F32)
    sums = jnp.dot(ld_ref[0], upper, precision=HIGH, preferred_element_type=F32) * LOG2E
    for slot in range(slots):
        count = min(n, heads - slot * n)
        lds[0:count, slot, 0:tok] = sums[slot * n : slot * n + count]
    ldr[me] = lds[me]

    def x_slot(slot):
        for p in range(n // 2):
            h = slot * n + 2 * p
            if h < heads:
                t = x_ref[0, :, h * dim : (h + 2) * dim]
                top, bot = t[:half], t[half:]
                xs[2 * p, slot] = lanes(top[:, :dim], bot[:, :dim])
                xs[2 * p + 1, slot] = lanes(top[:, dim:], bot[:, dim:])
            else:
                xs[2 * p, slot] = jnp.zeros((half, 2 * dim), BF16)
                xs[2 * p + 1, slot] = jnp.zeros((half, 2 * dim), BF16)
        xr[me, slot] = xs[me, slot]

    def qk_slot():
        for which, src in enumerate((q_ref, k_ref)):
            for p in range(per * n // 2):
                t = src[0, :, p * 2 * dim : (p + 1) * 2 * dim]
                top, bot = t[:half], t[half:]
                h = 2 * p
                qks[h % n, 2 * (h // n) + which] = lanes(top[:, :dim], bot[:, :dim])
                h = 2 * p + 1
                qks[h % n, 2 * (h // n) + which] = lanes(top[:, dim:], bot[:, dim:])
        qkr[me] = qks[me]

    loads[3].wait()
    x_slot(0)
    pl.semaphore_wait(barrier, n - 1)
    evens(lambda k: bc_copy(k).start())
    bc_partner().start()
    start(ld_copy)
    start(x_copy(0))
    loads[4].wait()
    loads[5].wait()
    qk_slot()
    start(qk_copy)
    evens(bc_relay)
    for slot in range(1, slots):
        x_slot(slot)
        start(x_copy(slot))

    def unpack(ref, index):
        parts = []
        for c in range(n):
            t = ref[c, index]
            parts += [t[:, :dim], t[:, dim:]]
        return rows(parts)

    def packed(a):
        return lanes(a[:half], a[half:])

    bc_partner().wait_recv()
    evens(lambda k: bc_forward(k).wait_recv())
    b_all = bcr[:, 0:tok, :].reshape(length, bcr.shape[2])
    for i in range(nblk):
        if blk % tok == 0:
            c_i = bcr[i * (blk // tok) : (i + 1) * (blk // tok), tok:, :].reshape(blk, bcr.shape[2])
        inner[i * blk : (i + 1) * blk, 0 : (i + 1) * blk] = lax.dot_general(
            c_i, b_all[: (i + 1) * blk], (((1,), (1,)), ((), ())), preferred_element_type=F32)
    arrive(ld_copy)
    offset = jnp.zeros((ldr.shape[1], 1), F32)
    parts = []
    for c in range(n):
        part = ldr[c][:, :tok] + offset
        offset = part[:, tok - 1 : tok]
        parts.append(part)
    cum = jnp.concatenate(parts, axis=1)
    cum_t = cum.T
    loads[6].wait()

    lower = (lax.broadcasted_iota(jnp.int32, (blk, blk), 0)
             >= lax.broadcasted_iota(jnp.int32, (blk, blk), 1))

    def attend(slot, values):
        q = unpack(qkr, 2 * slot)
        key = unpack(qkr, 2 * slot + 1)
        for i in range(nblk):
            s = lax.dot_general(q[i * blk : (i + 1) * blk], key[: (i + 1) * blk],
                                (((1,), (1,)), ((), ())), preferred_element_type=F32)
            s = s * (dim ** -0.5 * LOG2E)
            diag = jnp.where(lower, s[:, i * blk :], -jnp.inf)
            s = diag if i == 0 else lanes(s[:, : i * blk], diag)
            top = jnp.max(s, axis=-1, keepdims=True)
            w = jnp.exp2(s - top)
            total = jnp.sum(w, axis=-1, keepdims=True)
            mixed = jnp.dot(w.astype(BF16), values[: (i + 1) * blk], preferred_element_type=F32) / total
            mixed = mixed.astype(BF16)
            for c in range(blk // tok):
                ats[i * (blk // tok) + c, slot] = packed(mixed[c * tok : (c + 1) * tok])

    for slot in range(slots):
        head = jnp.minimum(me + slot * n, heads - 1)
        arrive(x_copy(slot))
        x_all = unpack(xr, slot)
        skip = skip_ref[head]
        pair = gain_ref[pl.ds(head // 2, 1), :]
        gain = jnp.where(head % 2 == 0, pair[:, :dim], pair[:, dim:])
        outs = []
        for i in range(nblk):
            here = cum_t[i * blk : (i + 1) * blk, slot : slot + 1]
            w = here - cum[slot : slot + 1, : (i + 1) * blk]
            diag = jnp.where(lower, w[:, i * blk :], -jnp.inf)
            w = diag if i == 0 else lanes(w[:, : i * blk], diag)
            w = jnp.exp2(w) * inner[i * blk : (i + 1) * blk, : (i + 1) * blk]
            y = jnp.dot(w.astype(BF16), x_all[: (i + 1) * blk], preferred_element_type=F32)
            y = y + skip * x_all[i * blk : (i + 1) * blk].astype(F32)
            mean = jnp.mean(y * y, axis=-1, keepdims=True)
            y = (y * lax.rsqrt(mean + 1e-05) * gain).astype(BF16)
            for c in range(blk // tok):
                ys[i * (blk // tok) + c, slot] = packed(y[c * tok : (c + 1) * tok])
            outs.append(y)
        start(y_copy(slot))
        yr[me, slot] = ys[me, slot]
        if slot < per:
            if slot == 0:
                arrive(qk_copy)
            attend(slot, rows(outs))
            if slot == per - 1:
                start(att_copy)
                atr[me] = ats[me]

    def unpack_out(ref, slot, dst):
        for p in range(n // 2):
            h = slot * n + 2 * p
            if h * dim < dst.shape[2]:
                even, odd = ref[2 * p, slot], ref[2 * p + 1, slot]
                dst[0, :half, h * dim : (h + 2) * dim] = lanes(even[:, :dim], odd[:, :dim])
                dst[0, half:, h * dim : (h + 2) * dim] = lanes(even[:, dim:], odd[:, dim:])

    for slot in range(slots):
        arrive(y_copy(slot))
        unpack_out(yr, slot, out_ref)
        if slot == per - 1:
            arrive(att_copy)
            for a in range(per):
                unpack_out(atr, a, att_ref)

    bc_partner().wait_send()
    evens(lambda k: bc_copy(k).wait_send())
    evens(lambda k: bc_forward(k).wait_send())
    left(ld_copy)
    left(qk_copy)
    left(att_copy)
    for slot in range(slots):
        left(x_copy(slot))
        left(y_copy(slot))


def local(n, x_in, b_in, c_in, log_decay, skip, norm_gain, queries, keys):
    tok, width = x_in.shape[1:]
    heads = log_decay.shape[1]
    dim = width // heads
    state = b_in.shape[2]
    per = queries.shape[2] // dim // n
    slots = -(-heads // n)
    length = n * tok
    blk = 128 if length <= 512 else 256
    half = tok // 2
    pad = -(-slots // 8) * 8
    vmem = pl.BlockSpec(memory_space=pltpu.VMEM)
    hbm = pl.BlockSpec(memory_space=pltpu.HBM)
    smem = pl.BlockSpec(memory_space=pltpu.SMEM)
    block = lambda k: pltpu.VMEM((n, k, half, 2 * dim), BF16)
    rows_of = FIXED + 2 * slots
    return pl.pallas_call(
        functools.partial(kernel, n, tok, heads, dim, per, blk),
        out_shape=(jax.ShapeDtypeStruct(x_in.shape, BF16), jax.ShapeDtypeStruct(queries.shape, BF16)),
        in_specs=[hbm, hbm, hbm, hbm, smem, hbm, hbm, hbm],
        out_specs=(vmem, vmem),
        scratch_shapes=[
            pltpu.VMEM(x_in.shape, BF16), pltpu.VMEM(log_decay.shape, F32),
            pltpu.VMEM((width // (2 * dim), 2 * dim), F32), pltpu.VMEM(queries.shape, BF16),
            pltpu.VMEM(keys.shape, BF16), pltpu.SemaphoreType.DMA((7,)),
            block(slots), block(slots), block(2 * per), block(2 * per),
            pltpu.VMEM((2 * tok, state), BF16), pltpu.VMEM((n, 2 * tok, state), BF16),
            pltpu.VMEM((n, pad, 128), F32), pltpu.VMEM((n, pad, 128), F32),
            block(slots), block(slots), block(per), block(per),
            pltpu.VMEM((length, length), F32),
            pltpu.SemaphoreType.DMA((rows_of, n)), pltpu.SemaphoreType.DMA((rows_of, n)),
        ],
        compiler_params=pltpu.CompilerParams(
            collective_id=0, has_side_effects=True, vmem_limit_bytes=63 * 1024 * 1024),
    )(x_in, b_in, c_in, log_decay, skip, norm_gain.reshape(width // (2 * dim), 2 * dim), queries, keys)


def solution(mesh):
    rows_spec = P(("groups", "batch"), "seq", None)
    return jax.shard_map(
        functools.partial(local, mesh.shape["seq"]),
        mesh=mesh,
        in_specs=(rows_spec, rows_spec, rows_spec, P(("groups", "batch"), None, "seq"),
                  P(), P(), rows_spec, rows_spec),
        out_specs=(rows_spec, rows_spec),
        check_vma=False,
    )
```

```python
import functools
import math
import jax
import jax.numpy as jnp
from jax import lax
from jax.sharding import PartitionSpec as P
from jax.experimental import pallas as pl
from jax.experimental.pallas import tpu as pltpu

F32 = jnp.float32
BF16 = jnp.bfloat16
HIGH = lax.Precision.HIGHEST
LOG2E = math.log2(math.e)
MESH = pl.DeviceIdType.MESH
BC, LD, QK, ATT, FWD, FIXED = 0, 1, 2, 3, 4, 5


def lanes(a, b):
    return jnp.concatenate([a, b], axis=1)


def rows(parts):
    return jnp.concatenate(parts, axis=0)


def kernel(n, tok, heads, dim, per, blk,
           x_hbm, b_hbm, c_hbm, ld_hbm, skip_ref, gain_hbm, q_hbm, k_hbm,
           out_ref, att_ref,
           x_ref, ld_ref, gain_ref, q_ref, k_ref, load, xs, xr, qks, qkr, bcs, bcr, lds, ldr, ys, yr, ats, atr, inner, send, recv):
    me = lax.axis_index("seq")
    half = tok // 2
    slots = xs.shape[1]
    length = n * tok
    nblk = length // blk

    loads = [pltpu.make_async_copy(src, dst, load.at[i]) for i, (src, dst) in enumerate((
        (b_hbm.at[0], bcs.at[0:tok]), (c_hbm.at[0], bcs.at[tok : 2 * tok]), (ld_hbm, ld_ref), (x_hbm, x_ref),
        (q_hbm, q_ref), (k_hbm, k_ref), (gain_hbm, gain_ref)))]
    for one in loads:
        one.start()
    barrier = pltpu.get_barrier_semaphore()

    def greet(k, _):
        pl.semaphore_signal(barrier, inc=1, device_id={"seq": lax.rem(me + k, n)}, device_id_type=MESH)
        return 0

    lax.fori_loop(1, n, greet, 0)

    def copy(src, dst, row, k):
        return pltpu.make_async_remote_copy(
            src_ref=src, dst_ref=dst, send_sem=send.at[row, k], recv_sem=recv.at[row, k],
            device_id={"seq": lax.rem(me + k, n)}, device_id_type=MESH)

    def to(k):
        return lax.rem(me + k, n)

    def each(fn):
        def body(k, _):
            fn(k)
            return 0
        lax.fori_loop(1, n, body, 0)

    partner = me + 1 - 2 * lax.rem(me, 2)

    def bc_partner():
        return pltpu.make_async_remote_copy(
            src_ref=bcs, dst_ref=bcr.at[me], send_sem=send.at[BC, 1], recv_sem=recv.at[BC, 1],
            device_id={"seq": partner}, device_id_type=MESH)

    def bc_forward(k):
        slot = lax.rem(me + n - k, n)
        return pltpu.make_async_remote_copy(
            src_ref=bcr.at[slot], dst_ref=bcr.at[slot], send_sem=send.at[FWD, k], recv_sem=recv.at[FWD, k],
            device_id={"seq": partner}, device_id_type=MESH)

    def evens(fn):
        def body(j, _):
            fn(2 * j)
            return 0
        lax.fori_loop(1, n // 2, body, 0)

    def bc_relay(k):
        bc_copy(k).wait_recv()
        bc_forward(k).start()

    bc_copy = lambda k: copy(bcs, bcr.at[me], BC, k)
    ld_copy = lambda k: copy(lds.at[to(k)], ldr.at[me], LD, k)
    qk_copy = lambda k: copy(qks.at[to(k)], qkr.at[me], QK, k)
    att_copy = lambda k: copy(ats.at[to(k)], atr.at[me], ATT, k)
    x_copy = lambda slot: lambda k: copy(xs.at[to(k), slot], xr.at[me, slot], FIXED + slot, k)
    y_copy = lambda slot: lambda k: copy(ys.at[to(k), slot], yr.at[me, slot], FIXED + slots + slot, k)
    start = lambda mk: each(lambda k: mk(n - k).start())
    arrive = lambda mk: each(lambda k: mk(k).wait_recv())
    left = lambda mk: each(lambda k: mk(k).wait_send())

    lds[...] = jnp.zeros_like(lds)
    def x_slot(slot):
        for p in range(n // 2):
            h = slot * n + 2 * p
            if h < heads:
                t = x_ref[0, :, h * dim : (h + 2) * dim]
                top, bot = t[:half], t[half:]
                xs[2 * p, slot] = lanes(top[:, :dim], bot[:, :dim])
                xs[2 * p + 1, slot] = lanes(top[:, dim:], bot[:, dim:])
            else:
                xs[2 * p, slot] = jnp.zeros((half, 2 * dim), BF16)
                xs[2 * p + 1, slot] = jnp.zeros((half, 2 * dim), BF16)
        xr[me, slot] = xs[me, slot]

    def qk_slot():
        for which, src in enumerate((q_ref, k_ref)):
            for p in range(per * n // 2):
                t = src[0, :, p * 2 * dim : (p + 1) * 2 * dim]
                top, bot = t[:half], t[half:]
                h = 2 * p
                qks[h % n, 2 * (h // n) + which] = lanes(top[:, :dim], bot[:, :dim])
                h = 2 * p + 1
                qks[h % n, 2 * (h // n) + which] = lanes(top[:, dim:], bot[:, dim:])
        qkr[me] = qks[me]

    loads[3].wait()
    x_slot(0)
    loads[0].wait()
    loads[1].wait()
    pl.semaphore_wait(barrier, n - 1)
    evens(lambda k: bc_copy(n - k).start())
    bc_partner().start()
    start(x_copy(0))
    bcr[me] = bcs[...]
    loads[2].wait()
    upper = (lax.broadcasted_iota(jnp.int32, (tok, tok), 0)
             <= lax.broadcasted_iota(jnp.int32, (tok, tok), 1)).astype(F32)
    sums = jnp.dot(ld_ref[0], upper, precision=HIGH, preferred_element_type=F32) * LOG2E
    for slot in range(slots):
        count = min(n, heads - slot * n)
        lds[0:count, slot, 0:tok] = sums[slot * n : slot * n + count]
    ldr[me] = lds[me]

    start(ld_copy)
    loads[4].wait()
    loads[5].wait()
    qk_slot()
    start(qk_copy)
    evens(bc_relay)
    for slot in range(1, slots):
        x_slot(slot)
        start(x_copy(slot))

    def unpack(ref, index):
        parts = []
        for c in range(n):
            t = ref[c, index]
            parts += [t[:, :dim], t[:, dim:]]
        return rows(parts)

    def packed(a):
        return lanes(a[:half], a[half:])

    bc_partner().wait_recv()
    evens(lambda k: bc_forward(k).wait_recv())
    b_all = bcr[:, 0:tok, :].reshape(length, bcr.shape[2])
    for i in range(nblk):
        if blk % tok == 0:
            c_i = bcr[i * (blk // tok) : (i + 1) * (blk // tok), tok:, :].reshape(blk, bcr.shape[2])
        inner[i * blk : (i + 1) * blk, 0 : (i + 1) * blk] = lax.dot_general(
            c_i, b_all[: (i + 1) * blk], (((1,), (1,)), ((), ())), preferred_element_type=F32)
    arrive(ld_copy)
    offset = jnp.zeros((ldr.shape[1], 1), F32)
    parts = []
    for c in range(n):
        part = ldr[c][:, :tok] + offset
        offset = part[:, tok - 1 : tok]
        parts.append(part)
    cum = jnp.concatenate(parts, axis=1)
    cum_t = cum.T
    loads[6].wait()

    lower = (lax.broadcasted_iota(jnp.int32, (blk, blk), 0)
             >= lax.broadcasted_iota(jnp.int32, (blk, blk), 1))

    def attend(slot, values):
        q = unpack(qkr, 2 * slot)
        key = unpack(qkr, 2 * slot + 1)
        for i in range(nblk):
            s = lax.dot_general(q[i * blk : (i + 1) * blk], key[: (i + 1) * blk],
                                (((1,), (1,)), ((), ())), preferred_element_type=F32)
            s = s * (dim ** -0.5 * LOG2E)
            diag = jnp.where(lower, s[:, i * blk :], -jnp.inf)
            s = diag if i == 0 else lanes(s[:, : i * blk], diag)
            top = jnp.max(s, axis=-1, keepdims=True)
            w = jnp.exp2(s - top)
            total = jnp.sum(w, axis=-1, keepdims=True)
            mixed = jnp.dot(w.astype(BF16), values[: (i + 1) * blk], preferred_element_type=F32) / total
            mixed = mixed.astype(BF16)
            for c in range(blk // tok):
                ats[i * (blk // tok) + c, slot] = packed(mixed[c * tok : (c + 1) * tok])

    for slot in range(slots):
        head = jnp.minimum(me + slot * n, heads - 1)
        arrive(x_copy(slot))
        x_all = unpack(xr, slot)
        skip = skip_ref[head]
        pair = gain_ref[pl.ds(head // 2, 1), :]
        gain = jnp.where(head % 2 == 0, pair[:, :dim], pair[:, dim:])
        outs = []
        for i in range(nblk):
            here = cum_t[i * blk : (i + 1) * blk, slot : slot + 1]
            w = here - cum[slot : slot + 1, : (i + 1) * blk]
            diag = jnp.where(lower, w[:, i * blk :], -jnp.inf)
            w = diag if i == 0 else lanes(w[:, : i * blk], diag)
            w = jnp.exp2(w) * inner[i * blk : (i + 1) * blk, : (i + 1) * blk]
            y = jnp.dot(w.astype(BF16), x_all[: (i + 1) * blk], preferred_element_type=F32)
            y = y + skip * x_all[i * blk : (i + 1) * blk].astype(F32)
            mean = jnp.mean(y * y, axis=-1, keepdims=True)
            y = (y * lax.rsqrt(mean + 1e-05) * gain).astype(BF16)
            for c in range(blk // tok):
                ys[i * (blk // tok) + c, slot] = packed(y[c * tok : (c + 1) * tok])
            outs.append(y)
        start(y_copy(slot))
        yr[me, slot] = ys[me, slot]
        if slot < per:
            if slot == 0:
                arrive(qk_copy)
            attend(slot, rows(outs))
            if slot == per - 1:
                start(att_copy)
                atr[me] = ats[me]

    def unpack_out(ref, slot, dst):
        for p in range(n // 2):
            h = slot * n + 2 * p
            if h * dim < dst.shape[2]:
                even, odd = ref[2 * p, slot], ref[2 * p + 1, slot]
                dst[0, :half, h * dim : (h + 2) * dim] = lanes(even[:, :dim], odd[:, :dim])
                dst[0, half:, h * dim : (h + 2) * dim] = lanes(even[:, dim:], odd[:, dim:])

    for slot in range(slots):
        arrive(y_copy(slot))
        unpack_out(yr, slot, out_ref)
        if slot == per - 1:
            arrive(att_copy)
            for a in range(per):
                unpack_out(atr, a, att_ref)

    bc_partner().wait_send()
    evens(lambda k: bc_copy(k).wait_send())
    evens(lambda k: bc_forward(k).wait_send())
    left(ld_copy)
    left(qk_copy)
    left(att_copy)
    for slot in range(slots):
        left(x_copy(slot))
        left(y_copy(slot))


def local(n, x_in, b_in, c_in, log_decay, skip, norm_gain, queries, keys):
    tok, width = x_in.shape[1:]
    heads = log_decay.shape[1]
    dim = width // heads
    state = b_in.shape[2]
    per = queries.shape[2] // dim // n
    slots = -(-heads // n)
    length = n * tok
    blk = 128 if length <= 512 else 256
    half = tok // 2
    pad = -(-slots // 8) * 8
    vmem = pl.BlockSpec(memory_space=pltpu.VMEM)
    hbm = pl.BlockSpec(memory_space=pltpu.HBM)
    smem = pl.BlockSpec(memory_space=pltpu.SMEM)
    block = lambda k: pltpu.VMEM((n, k, half, 2 * dim), BF16)
    rows_of = FIXED + 2 * slots
    return pl.pallas_call(
        functools.partial(kernel, n, tok, heads, dim, per, blk),
        out_shape=(jax.ShapeDtypeStruct(x_in.shape, BF16), jax.ShapeDtypeStruct(queries.shape, BF16)),
        in_specs=[hbm, hbm, hbm, hbm, smem, hbm, hbm, hbm],
        out_specs=(vmem, vmem),
        scratch_shapes=[
            pltpu.VMEM(x_in.shape, BF16), pltpu.VMEM(log_decay.shape, F32),
            pltpu.VMEM((width // (2 * dim), 2 * dim), F32), pltpu.VMEM(queries.shape, BF16),
            pltpu.VMEM(keys.shape, BF16), pltpu.SemaphoreType.DMA((7,)),
            block(slots), block(slots), block(2 * per), block(2 * per),
            pltpu.VMEM((2 * tok, state), BF16), pltpu.VMEM((n, 2 * tok, state), BF16),
            pltpu.VMEM((n, pad, 128), F32), pltpu.VMEM((n, pad, 128), F32),
            block(slots), block(slots), block(per), block(per),
            pltpu.VMEM((length, length), F32),
            pltpu.SemaphoreType.DMA((rows_of, n)), pltpu.SemaphoreType.DMA((rows_of, n)),
        ],
        compiler_params=pltpu.CompilerParams(
            collective_id=0, has_side_effects=True, vmem_limit_bytes=63 * 1024 * 1024),
    )(x_in, b_in, c_in, log_decay, skip, norm_gain.reshape(width // (2 * dim), 2 * dim), queries, keys)


def solution(mesh):
    rows_spec = P(("groups", "batch"), "seq", None)
    return jax.shard_map(
        functools.partial(local, mesh.shape["seq"]),
        mesh=mesh,
        in_specs=(rows_spec, rows_spec, rows_spec, P(("groups", "batch"), None, "seq"),
                  P(), P(), rows_spec, rows_spec),
        out_specs=(rows_spec, rows_spec),
        check_vma=False,
    )
```

```python
import functools
import math
import jax
import jax.numpy as jnp
from jax import lax
from jax.sharding import PartitionSpec as P
from jax.experimental import pallas as pl
from jax.experimental.pallas import tpu as pltpu

F32 = jnp.float32
BF16 = jnp.bfloat16
HIGH = lax.Precision.HIGHEST
LOG2E = math.log2(math.e)
MESH = pl.DeviceIdType.MESH
BC, LD, QK, ATT, FWD, FIXED = 0, 1, 2, 3, 4, 5


def lanes(a, b):
    return jnp.concatenate([a, b], axis=1)


def rows(parts):
    return jnp.concatenate(parts, axis=0)


def kernel(n, tok, heads, dim, per, blk,
           x_hbm, b_hbm, c_hbm, ld_hbm, skip_ref, gain_hbm, q_hbm, k_hbm,
           out_ref, att_ref,
           x_ref, ld_ref, gain_ref, q_ref, k_ref, load, xs, xr, qks, qkr, bcs, bcr, lds, ldr, ys, yr, ats, atr, inner, send, recv):
    me = lax.axis_index("seq")
    half = tok // 2
    slots = xs.shape[1]
    length = n * tok
    nblk = length // blk

    loads = [pltpu.make_async_copy(src, dst, load.at[i]) for i, (src, dst) in enumerate((
        (b_hbm.at[0], bcs.at[0:tok]), (c_hbm.at[0], bcs.at[tok : 2 * tok]), (ld_hbm, ld_ref), (x_hbm, x_ref),
        (q_hbm, q_ref), (k_hbm, k_ref), (gain_hbm, gain_ref)))]
    for one in loads:
        one.start()
    barrier = pltpu.get_barrier_semaphore()

    def greet(k, _):
        pl.semaphore_signal(barrier, inc=1, device_id={"seq": lax.rem(me + k, n)}, device_id_type=MESH)
        return 0

    lax.fori_loop(1, n, greet, 0)

    def copy(src, dst, row, k):
        return pltpu.make_async_remote_copy(
            src_ref=src, dst_ref=dst, send_sem=send.at[row, k], recv_sem=recv.at[row, k],
            device_id={"seq": lax.rem(me + k, n)}, device_id_type=MESH)

    def to(k):
        return lax.rem(me + k, n)

    def each(fn):
        def body(k, _):
            fn(k)
            return 0
        lax.fori_loop(1, n, body, 0, unroll=n <= 8)

    partner = me + 1 - 2 * lax.rem(me, 2)

    def bc_partner():
        return pltpu.make_async_remote_copy(
            src_ref=bcs, dst_ref=bcr.at[me], send_sem=send.at[BC, 1], recv_sem=recv.at[BC, 1],
            device_id={"seq": partner}, device_id_type=MESH)

    def bc_forward(k):
        slot = lax.rem(me + n - k, n)
        return pltpu.make_async_remote_copy(
            src_ref=bcr.at[slot], dst_ref=bcr.at[slot], send_sem=send.at[FWD, k], recv_sem=recv.at[FWD, k],
            device_id={"seq": partner}, device_id_type=MESH)

    def evens(fn):
        def body(j, _):
            fn(2 * j)
            return 0
        lax.fori_loop(1, n // 2, body, 0, unroll=n <= 8)

    def bc_relay(k):
        bc_copy(k).wait_recv()
        bc_forward(k).start()

    bc_copy = lambda k: copy(bcs, bcr.at[me], BC, k)
    ld_copy = lambda k: copy(lds.at[to(k)], ldr.at[me], LD, k)
    qk_copy = lambda k: copy(qks.at[to(k)], qkr.at[me], QK, k)
    att_copy = lambda k: copy(ats.at[to(k)], atr.at[me], ATT, k)
    x_copy = lambda slot: lambda k: copy(xs.at[to(k), slot], xr.at[me, slot], FIXED + slot, k)
    y_copy = lambda slot: lambda k: copy(ys.at[to(k), slot], yr.at[me, slot], FIXED + slots + slot, k)
    start = lambda mk: each(lambda k: mk(n - k).start())
    arrive = lambda mk: each(lambda k: mk(k).wait_recv())
    left = lambda mk: each(lambda k: mk(k).wait_send())

    lds[...] = jnp.zeros_like(lds)
    def x_slot(slot):
        for p in range(n // 2):
            h = slot * n + 2 * p
            if h < heads:
                t = x_ref[0, :, h * dim : (h + 2) * dim]
                top, bot = t[:half], t[half:]
                xs[2 * p, slot] = lanes(top[:, :dim], bot[:, :dim])
                xs[2 * p + 1, slot] = lanes(top[:, dim:], bot[:, dim:])
            else:
                xs[2 * p, slot] = jnp.zeros((half, 2 * dim), BF16)
                xs[2 * p + 1, slot] = jnp.zeros((half, 2 * dim), BF16)
        xr[me, slot] = xs[me, slot]

    def qk_slot():
        for which, src in enumerate((q_ref, k_ref)):
            for p in range(per * n // 2):
                t = src[0, :, p * 2 * dim : (p + 1) * 2 * dim]
                top, bot = t[:half], t[half:]
                h = 2 * p
                qks[h % n, 2 * (h // n) + which] = lanes(top[:, :dim], bot[:, :dim])
                h = 2 * p + 1
                qks[h % n, 2 * (h // n) + which] = lanes(top[:, dim:], bot[:, dim:])
        qkr[me] = qks[me]

    loads[3].wait()
    x_slot(0)
    loads[0].wait()
    loads[1].wait()
    pl.semaphore_wait(barrier, n - 1)
    evens(lambda k: bc_copy(n - k).start())
    bc_partner().start()
    start(x_copy(0))
    bcr[me] = bcs[...]
    loads[2].wait()
    upper = (lax.broadcasted_iota(jnp.int32, (tok, tok), 0)
             <= lax.broadcasted_iota(jnp.int32, (tok, tok), 1)).astype(F32)
    sums = jnp.dot(ld_ref[0], upper, precision=HIGH, preferred_element_type=F32) * LOG2E
    for slot in range(slots):
        count = min(n, heads - slot * n)
        lds[0:count, slot, 0:tok] = sums[slot * n : slot * n + count]
    ldr[me] = lds[me]

    start(ld_copy)
    loads[4].wait()
    loads[5].wait()
    qk_slot()
    start(qk_copy)
    evens(bc_relay)
    for slot in range(1, slots):
        x_slot(slot)
        start(x_copy(slot))

    def unpack(ref, index):
        parts = []
        for c in range(n):
            t = ref[c, index]
            parts += [t[:, :dim], t[:, dim:]]
        return rows(parts)

    def packed(a):
        return lanes(a[:half], a[half:])

    bc_partner().wait_recv()
    evens(lambda k: bc_forward(k).wait_recv())
    b_all = bcr[:, 0:tok, :].reshape(length, bcr.shape[2])
    for i in range(nblk):
        if blk % tok == 0:
            c_i = bcr[i * (blk // tok) : (i + 1) * (blk // tok), tok:, :].reshape(blk, bcr.shape[2])
        inner[i * blk : (i + 1) * blk, 0 : (i + 1) * blk] = lax.dot_general(
            c_i, b_all[: (i + 1) * blk], (((1,), (1,)), ((), ())), preferred_element_type=F32)
    arrive(ld_copy)
    offset = jnp.zeros((ldr.shape[1], 1), F32)
    parts = []
    for c in range(n):
        part = ldr[c][:, :tok] + offset
        offset = part[:, tok - 1 : tok]
        parts.append(part)
    cum = jnp.concatenate(parts, axis=1)
    cum_t = cum.T
    loads[6].wait()

    lower = (lax.broadcasted_iota(jnp.int32, (blk, blk), 0)
             >= lax.broadcasted_iota(jnp.int32, (blk, blk), 1))

    def attend(slot, values):
        q = unpack(qkr, 2 * slot)
        key = unpack(qkr, 2 * slot + 1)
        for i in range(nblk):
            s = lax.dot_general(q[i * blk : (i + 1) * blk], key[: (i + 1) * blk],
                                (((1,), (1,)), ((), ())), preferred_element_type=F32)
            s = s * (dim ** -0.5 * LOG2E)
            diag = jnp.where(lower, s[:, i * blk :], -jnp.inf)
            s = diag if i == 0 else lanes(s[:, : i * blk], diag)
            top = jnp.max(s, axis=-1, keepdims=True)
            w = jnp.exp2(s - top)
            total = jnp.sum(w, axis=-1, keepdims=True)
            mixed = jnp.dot(w.astype(BF16), values[: (i + 1) * blk], preferred_element_type=F32) / total
            mixed = mixed.astype(BF16)
            for c in range(blk // tok):
                ats[i * (blk // tok) + c, slot] = packed(mixed[c * tok : (c + 1) * tok])

    for slot in range(slots):
        head = jnp.minimum(me + slot * n, heads - 1)
        arrive(x_copy(slot))
        x_all = unpack(xr, slot)
        skip = skip_ref[head]
        pair = gain_ref[pl.ds(head // 2, 1), :]
        gain = jnp.where(head % 2 == 0, pair[:, :dim], pair[:, dim:])
        outs = []
        for i in range(nblk):
            here = cum_t[i * blk : (i + 1) * blk, slot : slot + 1]
            w = here - cum[slot : slot + 1, : (i + 1) * blk]
            diag = jnp.where(lower, w[:, i * blk :], -jnp.inf)
            w = diag if i == 0 else lanes(w[:, : i * blk], diag)
            w = jnp.exp2(w) * inner[i * blk : (i + 1) * blk, : (i + 1) * blk]
            y = jnp.dot(w.astype(BF16), x_all[: (i + 1) * blk], preferred_element_type=F32)
            y = y + skip * x_all[i * blk : (i + 1) * blk].astype(F32)
            mean = jnp.mean(y * y, axis=-1, keepdims=True)
            y = (y * lax.rsqrt(mean + 1e-05) * gain).astype(BF16)
            for c in range(blk // tok):
                ys[i * (blk // tok) + c, slot] = packed(y[c * tok : (c + 1) * tok])
            outs.append(y)
        start(y_copy(slot))
        yr[me, slot] = ys[me, slot]
        if slot < per:
            if slot == 0:
                arrive(qk_copy)
            attend(slot, rows(outs))
            if slot == per - 1:
                start(att_copy)
                atr[me] = ats[me]

    def unpack_out(ref, slot, dst):
        for p in range(n // 2):
            h = slot * n + 2 * p
            if h * dim < dst.shape[2]:
                even, odd = ref[2 * p, slot], ref[2 * p + 1, slot]
                dst[0, :half, h * dim : (h + 2) * dim] = lanes(even[:, :dim], odd[:, :dim])
                dst[0, half:, h * dim : (h + 2) * dim] = lanes(even[:, dim:], odd[:, dim:])

    for slot in range(slots):
        arrive(y_copy(slot))
        unpack_out(yr, slot, out_ref)
        if slot == per - 1:
            arrive(att_copy)
            for a in range(per):
                unpack_out(atr, a, att_ref)

    bc_partner().wait_send()
    evens(lambda k: bc_copy(k).wait_send())
    evens(lambda k: bc_forward(k).wait_send())
    left(ld_copy)
    left(qk_copy)
    left(att_copy)
    for slot in range(slots):
        left(x_copy(slot))
        left(y_copy(slot))


def local(n, x_in, b_in, c_in, log_decay, skip, norm_gain, queries, keys):
    tok, width = x_in.shape[1:]
    heads = log_decay.shape[1]
    dim = width // heads
    state = b_in.shape[2]
    per = queries.shape[2] // dim // n
    slots = -(-heads // n)
    length = n * tok
    blk = 128 if length <= 512 else 256
    half = tok // 2
    pad = -(-slots // 8) * 8
    vmem = pl.BlockSpec(memory_space=pltpu.VMEM)
    hbm = pl.BlockSpec(memory_space=pltpu.HBM)
    smem = pl.BlockSpec(memory_space=pltpu.SMEM)
    block = lambda k: pltpu.VMEM((n, k, half, 2 * dim), BF16)
    rows_of = FIXED + 2 * slots
    return pl.pallas_call(
        functools.partial(kernel, n, tok, heads, dim, per, blk),
        out_shape=(jax.ShapeDtypeStruct(x_in.shape, BF16), jax.ShapeDtypeStruct(queries.shape, BF16)),
        in_specs=[hbm, hbm, hbm, hbm, smem, hbm, hbm, hbm],
        out_specs=(vmem, vmem),
        scratch_shapes=[
            pltpu.VMEM(x_in.shape, BF16), pltpu.VMEM(log_decay.shape, F32),
            pltpu.VMEM((width // (2 * dim), 2 * dim), F32), pltpu.VMEM(queries.shape, BF16),
            pltpu.VMEM(keys.shape, BF16), pltpu.SemaphoreType.DMA((7,)),
            block(slots), block(slots), block(2 * per), block(2 * per),
            pltpu.VMEM((2 * tok, state), BF16), pltpu.VMEM((n, 2 * tok, state), BF16),
            pltpu.VMEM((n, pad, 128), F32), pltpu.VMEM((n, pad, 128), F32),
            block(slots), block(slots), block(per), block(per),
            pltpu.VMEM((length, length), F32),
            pltpu.SemaphoreType.DMA((rows_of, n)), pltpu.SemaphoreType.DMA((rows_of, n)),
        ],
        compiler_params=pltpu.CompilerParams(
            collective_id=0, has_side_effects=True, vmem_limit_bytes=63 * 1024 * 1024),
    )(x_in, b_in, c_in, log_decay, skip, norm_gain.reshape(width // (2 * dim), 2 * dim), queries, keys)


def solution(mesh):
    rows_spec = P(("groups", "batch"), "seq", None)
    return jax.shard_map(
        functools.partial(local, mesh.shape["seq"]),
        mesh=mesh,
        in_specs=(rows_spec, rows_spec, rows_spec, P(("groups", "batch"), None, "seq"),
                  P(), P(), rows_spec, rows_spec),
        out_specs=(rows_spec, rows_spec),
        check_vma=False,
    )
```
